32 devices in a mesh: rep: 2 (over y), fsdp: 8 (over z, core), adapt: 2 (over x), sub: 1.
Axes of the slice: x: 2, y: 2, z: 4, core: 2. Of those that a mesh axis runs over, the one named last changes fastest.
Arguments:
- tokens: bfloat16 [2, 2048, 8192], P('adapt', ('rep', 'fsdp', 'sub')), parts along dimension 1, may hold values from -6 to 6
- frozen_key_weight: bfloat16 [8192, 512], P('fsdp'), may hold values from -0.0625 to 0.0625
- adapter_down_maps: float32 [2, 8, 8192, 16], P('adapt', 'rep', 'fsdp'), parts along dimension 1, may hold values from -0.0625 to 0.0625
- adapter_up_maps: float32 [2, 8, 16, 512], P('adapt', 'rep'), parts along dimension 1, may hold values from -0.9 to 0.9
- tenant_of_block: int32 [2, 32], P('adapt', ('rep', 'fsdp', 'sub')), parts along dimension 1, may hold values from 0 to 3, as said below
- adapter_of_tenant: int32 [2, 8], P('adapt', 'rep'), parts along dimension 1, may hold values from 0 to 3
- cotangent: bfloat16 [2, 2048, 512], P('adapt', ('rep', 'fsdp', 'sub')), parts along dimension 1, may hold values from -6 to 6
Outputs:
- projected: bfloat16 [2, 2048, 512], P('adapt', ('rep', 'fsdp', 'sub')), parts along dimension 1
- token_input_gradient: bfloat16 [2, 2048, 8192], P('adapt', ('rep', 'fsdp', 'sub')), parts along dimension 1
- down_map_gradient: float32 [2, 8, 8192, 16], P('adapt', 'rep', ('fsdp', 'sub')), parts along dimension 1
- up_gradient_swapped: float32 [2, 8, 512, 16], P('adapt', 'rep', ('fsdp', 'sub')), parts along dimension 1
The draws below stay inside these ranges and needn't reach their ends.
There are 2 independent parts, one for each index of `rep`. The reference program is written for one: setup_inputs(seed, part) draws one part's arguments, and reference() takes and returns one part's arrays. A program takes and returns all parts, laid end to end along the dimension named above; an argument that names none is the same for every part. Nothing has to cross between parts.
Inputs may be any that keep to these rules, and one draw needn't show every extreme that they name: `tenant_of_block`: in each group every tenant owns exactly 256 rows, that is 4 blocks.
All inputs are finite; a program needn't handle non-finite values.
Results may differ from the reference program's by a relative error of at most 0.001.
Values may be sent and summed in bfloat16 or wider, within the bound.
A program may use at most 64 MiB of HBM per device.

```python
import jax
import jax.numpy as jnp
from jax import lax

MODEL_WIDTH = 8192
KEY_OUTPUT_WIDTH = 512
ADAPTER_RANK = 16
GROUP_SLOTS = 4
TEN_GROUP = 4
BLOCK = 64
GROUP_ROWS = 1024
GROUP_BLOCKS = 16
N_ADAPT = 2


def draw_tenant_of_block(key, part):
    key = jax.random.fold_in(key, 11)
    keys = jax.random.split(key, N_ADAPT)
    order = jax.vmap(lambda k: jax.random.permutation(k, GROUP_BLOCKS))(keys)
    return (order // (GROUP_BLOCKS // TEN_GROUP)).astype(jnp.int32)


def set_ends(values, rng, least, largest):
    shape = values.shape
    spot = [jax.random.randint(jax.random.fold_in(rng, axis), (), 0, shape[axis]) for axis in range(len(shape))]
    values = values.at[tuple(spot)].set(least)
    longest = shape.index(max(shape))
    spot[longest] = (spot[longest] + 1) % shape[longest]
    return values.at[tuple(spot)].set(largest)


def spiked(values, stream_key, source, target, blocks, factor):
    owner, partner = [(jnp.arange(values.shape[axis_at]) // (values.shape[axis_at] // blocks)).reshape([-1 if axis == axis_at else 1 for axis in range(values.ndim)]) for axis_at in (source, target)]
    chosen = jax.random.permutation(stream_key, blocks)[partner]
    strong = (owner == chosen) | (owner == (partner + blocks // 2) % blocks)
    return jnp.where(strong, factor * values, values)


def block_levels(stream_key, shape, cuts, least, largest):
    def one(axis_at, shards_of):
        steps = jax.random.uniform(jax.random.fold_in(jax.random.fold_in(stream_key, 6), axis_at), (shards_of,), jnp.float32, least / len(cuts), largest / len(cuts))
        return jnp.repeat(jnp.exp(steps), shape[axis_at] // shards_of).reshape((-1,) + (1,) * (len(shape) - axis_at - 1))

    level = one(*cuts[0])
    for cut in cuts[1:]:
        level = level * one(*cut)
    return level


def bell_draw(rng, dims, spread, bound, shards=(), kind=jnp.bfloat16):
    drawn = jax.random.normal(rng, dims, jnp.float32) * spread
    if len(shards) > 0:
        drawn = block_levels(rng, dims, shards, -0.22, 0.18) * drawn
    return jnp.clip(drawn, min=-bound, max=bound).astype(kind)


def heavy_noise(own_key, extent, width, bound, shards, heavy, held_as=jnp.bfloat16):
    array = width * jax.random.normal(own_key, extent, jnp.float32)
    if shards:
        array = array * block_levels(own_key, extent, shards, -0.22, 0.18)
    return jnp.clip(spiked(array, jax.random.fold_in(own_key, 3), *heavy), -bound, bound).astype(held_as)


def setup_inputs(seed: int = 0, part: int = 0) -> dict:
    key_of = jax.random.split(jax.random.key(seed), 8)
    own_keys = jax.random.split(jax.random.fold_in(key_of[7], part), 8)
    return {
        "tokens": heavy_noise(own_keys[0], (N_ADAPT, GROUP_ROWS, MODEL_WIDTH), 1.0, 6.0, ((0, 2), (1, 8)), (1, 2, 8, 2.0)),
        "frozen_key_weight": bell_draw(key_of[1], (MODEL_WIDTH, KEY_OUTPUT_WIDTH), MODEL_WIDTH ** -0.5, 0.0625, ((0, 8),)),
        "adapter_down_maps": bell_draw(own_keys[2], (N_ADAPT, GROUP_SLOTS, MODEL_WIDTH, ADAPTER_RANK), MODEL_WIDTH ** -0.5, 0.0625, ((0, 2), (2, 8)), jnp.float32),
        "adapter_up_maps": bell_draw(own_keys[3], (N_ADAPT, GROUP_SLOTS, ADAPTER_RANK, KEY_OUTPUT_WIDTH), 0.15, 0.9, ((0, 2),), jnp.float32),
        "tenant_of_block": draw_tenant_of_block(jax.random.fold_in(jax.random.fold_in(key_of[7], part), 71), part),
        "adapter_of_tenant": set_ends(jax.random.randint(own_keys[5], (N_ADAPT, TEN_GROUP), 0, GROUP_SLOTS), jax.random.fold_in(own_keys[5], 1), 0, GROUP_SLOTS - 1).astype(jnp.int32),
        "cotangent": bell_draw(own_keys[6], (N_ADAPT, GROUP_ROWS, KEY_OUTPUT_WIDTH), 1.0, 6.0, ((0, 2), (1, 8))),
    }


HIGH_PRECISION = lax.Precision.HIGHEST
adapter_scale = 2.0


def single_group_step(tokens, adapter_down_maps, adapter_up_maps, tenant_of_block, adapter_of_tenant, cotangent, frozen_key_weight):
    tenant_ids = jnp.arange(TEN_GROUP, dtype=jnp.int32)
    slot_block = jnp.sum(jnp.where(tenant_of_block[:, None] == tenant_ids[None, :], adapter_of_tenant[None, :], 0), axis=1).astype(jnp.int32)
    slot_row = jnp.repeat(slot_block, BLOCK)
    lanes = (jnp.arange(GROUP_SLOTS * ADAPTER_RANK, dtype=jnp.int32) // ADAPTER_RANK).astype(jnp.int32)
    slot_selection = (slot_row[:, None] == lanes[None, :]).astype(jnp.float32)
    down_flattened = jnp.transpose(adapter_down_maps, (1, 0, 2)).reshape(MODEL_WIDTH, GROUP_SLOTS * ADAPTER_RANK)
    up_flattened = adapter_up_maps.reshape(GROUP_SLOTS * ADAPTER_RANK, KEY_OUTPUT_WIDTH)
    feats32 = tokens.astype(jnp.float32)
    frozen_output = jnp.dot(tokens, frozen_key_weight, preferred_element_type=jnp.float32)
    low_rank_output = jnp.dot(feats32, down_flattened, precision=HIGH_PRECISION) * slot_selection
    projected = (frozen_output + adapter_scale * jnp.dot(low_rank_output, up_flattened, precision=HIGH_PRECISION)).astype(jnp.bfloat16)
    gradient_float32 = cotangent.astype(jnp.float32)
    low_rank_gradient = adapter_scale * jnp.dot(gradient_float32, up_flattened.T, precision=HIGH_PRECISION) * slot_selection
    up_gradient_flattened = adapter_scale * jnp.dot(gradient_float32.T, low_rank_output, precision=HIGH_PRECISION)
    grad_a_flat = jnp.dot(feats32.T, low_rank_gradient, precision=HIGH_PRECISION)
    back = jnp.dot(cotangent, frozen_key_weight.T, preferred_element_type=jnp.float32)
    token_input_gradient = (back + jnp.dot(low_rank_gradient, down_flattened.T, precision=HIGH_PRECISION)).astype(jnp.bfloat16)
    down_map_gradient = jnp.transpose(grad_a_flat.reshape(MODEL_WIDTH, GROUP_SLOTS, ADAPTER_RANK), (1, 0, 2))
    up_gradient_swapped = jnp.transpose(up_gradient_flattened.reshape(KEY_OUTPUT_WIDTH, GROUP_SLOTS, ADAPTER_RANK), (1, 0, 2))
    return projected, token_input_gradient, down_map_gradient, up_gradient_swapped


def reference(tokens, frozen_key_weight, adapter_down_maps, adapter_up_maps, tenant_of_block, adapter_of_tenant, cotangent):
    def training_update(items):
        return single_group_step(items[0], items[1], items[2], items[3], items[4], items[5], frozen_key_weight)

    projected, token_input_gradient, down_map_gradient, up_gradient_swapped = lax.map(training_update, (tokens, adapter_down_maps, adapter_up_maps, tenant_of_block, adapter_of_tenant, cotangent))
    return (projected, token_input_gradient, down_map_gradient, up_gradient_swapped)
```

```python
import functools

import jax
import jax.numpy as jnp
from jax import lax
from jax.experimental import pallas as pl
from jax.experimental.pallas import tpu as pltpu
from jax.sharding import PartitionSpec as P

HIGH_PRECISION = lax.Precision.HIGHEST
adapter_scale = 2.0


def per_device(
    tokens,
    frozen_key_weight,
    adapter_down_maps,
    adapter_up_maps,
    tenant_of_block,
    adapter_of_tenant,
    cotangent,
):
    feats = tokens[0]
    grad_out = cotangent[0]
    owners = tenant_of_block[0]
    slot_table = adapter_of_tenant[0]
    rows = feats.shape[0]
    width = feats.shape[1]
    output_width = frozen_key_weight.shape[1]
    slot_count = adapter_down_maps.shape[1]
    adapter_rank_value = adapter_down_maps.shape[3]
    tenant_ids = jnp.arange(slot_table.shape[0], dtype=jnp.int32)
    slot_block = jnp.sum(
        jnp.where(owners[:, None] == tenant_ids[None, :], slot_table[None, :], 0), axis=1
    )
    slot_row = jnp.repeat(slot_block, rows // owners.shape[0])
    lanes = jnp.arange(slot_count * adapter_rank_value, dtype=jnp.int32) // adapter_rank_value
    slot_selection = (slot_row[:, None] == lanes[None, :]).astype(jnp.float32)
    complete_down_maps = lax.all_gather(adapter_down_maps, "fsdp", axis=2, tiled=True)[0]
    down_flattened = jnp.transpose(complete_down_maps, (1, 0, 2)).reshape(
        width, slot_count * adapter_rank_value
    )
    up_flattened = adapter_up_maps[0].reshape(slot_count * adapter_rank_value, output_width)
    feats32 = feats.astype(jnp.float32)
    low_rank_output = jnp.dot(feats32, down_flattened, precision=HIGH_PRECISION) * slot_selection
    whole_weight = lax.all_gather(frozen_key_weight, "fsdp", axis=0, tiled=True)
    frozen_output = jnp.dot(feats, whole_weight, preferred_element_type=jnp.float32)
    projected = (
        frozen_output
        + adapter_scale * jnp.dot(low_rank_output, up_flattened, precision=HIGH_PRECISION)
    ).astype(jnp.bfloat16)
    gradient_float32 = grad_out.astype(jnp.float32)
    low_rank_gradient = (
        adapter_scale
        * jnp.dot(gradient_float32, up_flattened.T, precision=HIGH_PRECISION)
        * slot_selection
    )
    up_gradient_flattened = adapter_scale * jnp.dot(
        gradient_float32.T, low_rank_output, precision=HIGH_PRECISION
    )
    grad_a_flat = jnp.dot(feats32.T, low_rank_gradient, precision=HIGH_PRECISION)
    back = jnp.dot(grad_out, whole_weight.T, preferred_element_type=jnp.float32)
    token_input_gradient = (
        back + jnp.dot(low_rank_gradient, down_flattened.T, precision=HIGH_PRECISION)
    ).astype(jnp.bfloat16)
    grad_a_local = jnp.transpose(
        grad_a_flat.reshape(width, slot_count, adapter_rank_value), (1, 0, 2)
    )[None]
    grad_b_local = jnp.transpose(
        up_gradient_flattened.reshape(output_width, slot_count, adapter_rank_value), (1, 0, 2)
    )[None]
    down_map_gradient, up_gradient_swapped = (
        lax.psum_scatter(grad_a_local, ("fsdp", "sub"), scatter_dimension=2, tiled=True),
        lax.psum_scatter(grad_b_local, ("fsdp", "sub"), scatter_dimension=2, tiled=True),
    )
    return (projected[None], token_input_gradient[None], down_map_gradient, up_gradient_swapped)


CORES = 2
MESH = pl.DeviceIdType.MESH
bf16, f32 = jnp.bfloat16, jnp.float32


def halves(x):
    high = x.astype(bf16)
    low = (x - high.astype(f32)).astype(bf16)
    return high, low


def dot_nn(a, b):
    return lax.dot_general(a, b, (((1,), (0,)), ((), ())), preferred_element_type=f32)


def dot_nt(a, b):
    return lax.dot_general(a, b, (((1,), (1,)), ((), ())), preferred_element_type=f32)


def pick(z, values):
    out = values[-1]
    for i in range(len(values) - 2, -1, -1):
        out = jnp.where(z == i, values[i], out)
    return out


def step_kernel(
    chips,
    quarters,
    rank,
    tok_ref,
    w_ref,
    d_ref,
    up_ref,
    tenant_ref,
    slot_ref,
    cot_ref,
    proj_ref,
    tg_ref,
    dg_ref,
    ug_ref,
    wbuf,
    dbuf,
    gbuf,
    pbuf,
    rup,
    rdn,
    ubuf,
    urecv,
    dlc,
    acc,
    lacc,
    cw_s,
    cw_r,
    cd_s,
    cd_r,
    sd_s,
    sd_r,
    nb_s,
    nb_r,
    sb_s,
    sb_r,
    so_s,
    so_r,
    pr_s,
    pr_r,
    ch_s,
    up_r,
    dn_r,
    ug_s,
    ug_r,
    cp_s,
):
    me = lax.axis_index("fsdp")
    a = lax.axis_index("adapt")
    r = lax.axis_index("rep")
    n = chips * CORES
    z, c = me // CORES, me % CORES
    sib = z * CORES + (1 - c)
    quarter = r * 2 + a
    xq = r * 2 + (1 - a)
    yq = (1 - r) * 2 + a
    dq = (1 - r) * 2 + (1 - a)
    rows, width = tok_ref.shape
    depth = width // n
    cols = d_ref.shape[0]
    half = wbuf.shape[2] // 2
    upper, lower = z < chips - 1, z > 0
    SIB, XN, YN = {"fsdp": sib}, {"adapt": 1 - a}, {"rep": 1 - r}

    def at(zz, cc=None):
        return zz * CORES + (c if cc is None else cc)

    def rc(src, dst, ss, rs, dev):
        return pltpu.make_async_remote_copy(
            src_ref=src, dst_ref=dst, send_sem=ss, recv_sem=rs, device_id=dev, device_id_type=MESH
        )

    sends = []

    def send(cond, copy):
        if cond is None:
            copy.start()
            sends.append((None, copy))
        else:
            pl.when(cond)(copy.start)
            sends.append((cond, copy))

    def landed(dst, rs):
        rc(dst, dst, sb_s.at[0, 0], rs, SIB).wait_recv()

    own_w = pltpu.make_async_copy(w_ref, wbuf.at[me], cp_s)
    own_w.start()

    barrier = pltpu.get_barrier_semaphore()
    for i in range(1, n):
        pl.semaphore_signal(barrier, inc=1, device_id={"fsdp": lax.rem(me + i, n)}, device_id_type=MESH)
    pl.semaphore_signal(barrier, inc=1, device_id=XN, device_id_type=MESH)
    pl.semaphore_signal(barrier, inc=1, device_id=YN, device_id_type=MESH)

    d_hi, d_lo = halves(d_ref[...])
    dbuf[me, :cols] = d_hi
    dbuf[me, cols:] = d_lo
    own_w.wait()
    pl.semaphore_wait(barrier, n - 1 + 2)

    def chain_d(o_z, cond_up, cond_dn):
        ref = dbuf.at[at(o_z)]
        send(cond_up, rc(ref, ref, cd_s.at[0, o_z], cd_r.at[o_z], {"fsdp": at(z + 1)}))
        send(cond_dn, rc(ref, ref, cd_s.at[1, o_z], cd_r.at[o_z], {"fsdp": at(z - 1)}))
        send(None, rc(ref, ref, sd_s.at[o_z], sd_r.at[o_z], SIB))

    def chain_w(o_z, cond_up, cond_dn):
        ref = wbuf.at[at(o_z), quarter]
        send(cond_up, rc(ref, ref, cw_s.at[0, o_z], cw_r.at[o_z], {"fsdp": at(z + 1)}))
        send(cond_dn, rc(ref, ref, cw_s.at[1, o_z], cw_r.at[o_z], {"fsdp": at(z - 1)}))

    chain_d(z, upper, lower)
    chain_w(z, upper, lower)
    whole = wbuf.at[me]
    send(None, rc(whole, whole, so_s, so_r, SIB))

    owners = tenant_ref.shape[1]
    block = rows // owners
    row_at = lax.broadcasted_iota(jnp.int32, (cols, rows), 1) // block
    want = jnp.zeros((cols, rows), jnp.int32)
    for b in range(owners):
        t = tenant_ref[0, b]
        s = jnp.int32(0)
        for k in range(slot_ref.shape[1]):
            s = s + jnp.where(t == k, slot_ref[0, k], 0)
        want = jnp.where(row_at == b, s, want)
    have = lax.broadcasted_iota(jnp.int32, (cols, rows), 0) // rank
    select = jnp.where(have == want, 2.0, 0.0).astype(f32)
    up_hi, up_lo = halves(up_ref[...])
    cot = cot_ref[...]
    prod = dot_nt(jnp.concatenate([up_hi, up_lo], axis=0), cot)
    dl_hi, dl_lo = halves((prod[:cols] + prod[cols:]) * select)
    dl_hi32, dl_lo32 = dl_hi.astype(f32), dl_lo.astype(f32)
    dlt = jnp.concatenate([dl_hi, dl_lo], axis=0)
    dlc[0] = jnp.concatenate([dl_hi32, dl_lo32], axis=0).T.astype(bf16)
    dlc[1] = jnp.concatenate([dl_lo32, dl_hi32], axis=0).T.astype(bf16)

    def columns(o):
        return pl.ds(pl.multiple_of(o * depth, depth), depth)

    def grad_chunk(o):
        g = dot_nn(dlt, tok_ref[:, columns(o)])
        gbuf[o] = g[:cols] + g[cols:]

    turn = [pick(z, v) for v in ([3, 3, 0, 0], [2, 0, 3, 1], [1, 2, 1, 2], [0, 1, 2, 3])]
    origin = [pick(z, v) for v in ([1, 0, 3, 2], [2, 2, 1, 1], [3, 3, 0, 0])]

    for t in turn:
        grad_chunk(at(t, 1 - c))
        send(None, rc(gbuf.at[at(t, 1 - c)], pbuf.at[t], pr_s.at[t], pr_r.at[t], SIB))
    for t in turn:
        grad_chunk(at(t))

    def chain_g(t):
        landed(pbuf.at[t], pr_r.at[t])
        gbuf[at(t)] += pbuf[t]

        @pl.when((t > z) & lower)
        def _():
            landed(rup.at[t], up_r.at[t])
            gbuf[at(t)] += rup[t]

        @pl.when((t < z) & upper)
        def _():
            landed(rdn.at[t], dn_r.at[t])
            gbuf[at(t)] += rdn[t]

        src = gbuf.at[at(t)]
        send(t > z, rc(src, rup.at[t], ch_s.at[t], up_r.at[t], {"fsdp": at(z + 1)}))
        send(t < z, rc(src, rdn.at[t], ch_s.at[t], dn_r.at[t], {"fsdp": at(z - 1)}))

    def spread_w(o_z):
        ref = wbuf.at[at(o_z), quarter]
        send(None, rc(ref, ref, nb_s.at[0, o_z], nb_r.at[0, o_z], XN))
        send(None, rc(ref, ref, nb_s.at[1, o_z], nb_r.at[1, o_z], YN))
        send(None, rc(ref, ref, sb_s.at[0, o_z], sb_r.at[0, o_z], SIB))

    def swap_w(o_z):
        ref = wbuf.at[at(o_z), xq]
        landed(ref, nb_r.at[0, o_z])
        part = wbuf.at[at(o_z), xq, pl.ds(0, half)]
        send(None, rc(part, part, nb_s.at[2, o_z], nb_r.at[2, o_z], YN))
        send(None, rc(ref, ref, sb_s.at[1, o_z], sb_r.at[1, o_z], SIB))
        ref2 = wbuf.at[at(o_z), yq]
        landed(ref2, nb_r.at[1, o_z])
        part2 = wbuf.at[at(o_z), yq, pl.ds(half, half)]
        send(None, rc(part2, part2, nb_s.at[3, o_z], nb_r.at[3, o_z], XN))
        send(None, rc(ref2, ref2, sb_s.at[2, o_z], sb_r.at[2, o_z], SIB))

    def last_w(o_z):
        landed(wbuf.at[at(o_z), dq, pl.ds(0, half)], nb_r.at[2, o_z])
        landed(wbuf.at[at(o_z), dq, pl.ds(half, half)], nb_r.at[3, o_z])
        ref = wbuf.at[at(o_z), dq]
        send(None, rc(ref, ref, sb_s.at[3, o_z], sb_r.at[3, o_z], SIB))

    for j in range(chips - 1):
        o_z = origin[j]
        landed(dbuf.at[at(o_z)], cd_r.at[o_z])
        chain_d(o_z, (o_z < z) & upper, (o_z > z) & lower)
        landed(wbuf.at[at(o_z), quarter], cw_r.at[o_z])
        chain_w(o_z, (o_z < z) & upper, (o_z > z) & lower)
        spread_w(o_z)
        chain_g(turn[j])
        if j > 0:
            swap_w(origin[j - 1])

    for zz in range(chips):
        landed(dbuf.at[at(zz, 1 - c)], sd_r.at[zz])
    lacc[...] = jnp.zeros_like(lacc)

    @pl.loop(0, n)
    def _(o):
        lacc[...] += dot_nt(dbuf[o], tok_ref[:, columns(o)])

    low_hi, low_lo = halves((lacc[:cols] + lacc[cols:]) * select)
    lowc = jnp.concatenate([low_hi.astype(f32), low_lo.astype(f32)], axis=0).T.astype(bf16)
    cot_t = cot.astype(f32).T.astype(bf16)
    share = ubuf.shape[1]
    for f in range(n):
        ubuf[f] = dot_nn(cot_t[f * share : (f + 1) * share], lowc)
    for i in range(1, n):
        f = lax.rem(me + i, n)
        send(None, rc(ubuf.at[f], urecv.at[i], ug_s.at[i], ug_r.at[i], {"fsdp": f}))
    swap_w(origin[chips - 2])
    acc[...] = dot_nn(lowc, jnp.concatenate([up_hi, up_hi], axis=0)) + dot_nn(
        lowc, jnp.concatenate([up_lo, up_lo], axis=0)
    )

    def apply_w(o):
        w = wbuf[o].reshape(depth, wbuf.shape[3])
        acc[...] += dot_nn(tok_ref[:, columns(o)], w)
        d2 = dbuf[o]
        back = dot_nt(cot, w) + (dot_nn(dlc[0], d2) + dot_nn(dlc[1], d2))
        tg_ref[:, columns(o)] = back.astype(bf16)

    apply_w(me)
    landed(wbuf.at[sib], so_r)
    apply_w(sib)

    landed(pbuf.at[z], pr_r.at[z])
    dg_ref[...] = gbuf[me] + pbuf[z]

    @pl.when(lower)
    def _():
        landed(rup.at[z], up_r.at[z])
        dg_ref[...] += rup[z]

    @pl.when(upper)
    def _():
        landed(rdn.at[z], dn_r.at[z])
        dg_ref[...] += rdn[z]

    for j in range(chips - 1):
        o_z = origin[j]
        last_w(o_z)
        apply_w(at(o_z))
        for k, q in enumerate((quarter, xq, yq, dq)):
            landed(wbuf.at[at(o_z, 1 - c), q], sb_r.at[k, o_z])
        apply_w(at(o_z, 1 - c))

    total = ubuf[me]
    for i in range(1, n):
        landed(urecv.at[i], ug_r.at[i])
        total = total + urecv[i]
    ug_ref[...] = total
    proj_ref[...] = acc[...].astype(bf16)

    for cond, copy in sends:
        if cond is None:
            copy.wait_send()
        else:
            pl.when(cond)(copy.wait_send)


def fused_step(chips, tokens, weight, downs, ups, tenants, slots, cotangent):
    rows, width = tokens.shape[1:]
    depth, out_width = weight.shape
    slot_count, rank = downs.shape[1], downs.shape[3]
    cols = slot_count * rank
    n = chips * CORES
    quarters = 4
    share = out_width // n
    down_t = jnp.transpose(downs[0], (0, 2, 1)).reshape(cols, depth)
    dma = pltpu.SemaphoreType.DMA
    vmem = pl.BlockSpec(memory_space=pltpu.VMEM)
    smem = pl.BlockSpec(memory_space=pltpu.SMEM)
    proj, tg, dg, ug = pl.pallas_call(
        functools.partial(step_kernel, chips, quarters, rank),
        out_shape=(
            jax.ShapeDtypeStruct((rows, out_width), bf16),
            jax.ShapeDtypeStruct((rows, width), bf16),
            jax.ShapeDtypeStruct((cols, depth), f32),
            jax.ShapeDtypeStruct((share, 2 * cols), f32),
        ),
        in_specs=[vmem, pl.BlockSpec(memory_space=pl.ANY), vmem, vmem, smem, smem, vmem],
        out_specs=(vmem,) * 4,
        scratch_shapes=[
            pltpu.VMEM((n, quarters, depth // quarters, out_width), bf16),
            pltpu.VMEM((n, 2 * cols, depth), bf16),
            pltpu.VMEM((n, cols, depth), f32),
            pltpu.VMEM((chips, cols, depth), f32),
            pltpu.VMEM((chips, cols, depth), f32),
            pltpu.VMEM((chips, cols, depth), f32),
            pltpu.VMEM((n, share, 2 * cols), f32),
            pltpu.VMEM((n, share, 2 * cols), f32),
            pltpu.VMEM((2, rows, 2 * cols), bf16),
            pltpu.VMEM((rows, out_width), f32),
            pltpu.VMEM((2 * cols, rows), f32),
            dma((2, chips)),
            dma((chips,)),
            dma((2, chips)),
            dma((chips,)),
            dma((chips,)),
            dma((chips,)),
            dma((4, chips)),
            dma((4, chips)),
            dma((4, chips)),
            dma((4, chips)),
            dma,
            dma,
            dma((chips,)),
            dma((chips,)),
            dma((chips,)),
            dma((chips,)),
            dma((chips,)),
            dma((n,)),
            dma((n,)),
            dma,
        ],
        compiler_params=pltpu.CompilerParams(
            collective_id=0, has_side_effects=True, vmem_limit_bytes=48 * 1024 * 1024
        ),
        cost_estimate=pl.CostEstimate(
            flops=5 * rows * width * out_width, bytes_accessed=8 * 1024 * 1024, transcendentals=0
        ),
    )(
        tokens[0],
        weight.reshape(quarters, depth // quarters, out_width),
        down_t,
        ups[0].reshape(cols, out_width),
        tenants,
        slots,
        cotangent[0],
    )
    down_gradient = jnp.transpose(dg.reshape(slot_count, rank, depth), (0, 2, 1))[None]
    up_gradient = ug[:, :cols] + ug[:, cols:]
    up_gradient = jnp.transpose(up_gradient.reshape(share, slot_count, rank), (1, 0, 2))[None]
    return proj[None], tg[None], down_gradient, up_gradient


def solution(mesh):
    sizes = (mesh.shape["rep"], mesh.shape["fsdp"], mesh.shape["adapt"], mesh.shape["sub"])
    body = functools.partial(fused_step, sizes[1] // CORES) if sizes == (2, 8, 2, 1) else per_device
    in_specs = (
        P("adapt", ("rep", "fsdp", "sub"), None),
        P("fsdp", None),
        P("adapt", "rep", "fsdp", None),
        P("adapt", "rep", None, None),
        P("adapt", ("rep", "fsdp", "sub")),
        P("adapt", "rep"),
        P("adapt", ("rep", "fsdp", "sub"), None),
    )
    out_specs = (
        P("adapt", ("rep", "fsdp", "sub"), None),
        P("adapt", ("rep", "fsdp", "sub"), None),
        P("adapt", "rep", ("fsdp", "sub"), None),
        P("adapt", "rep", ("fsdp", "sub"), None),
    )
    return jax.shard_map(
        body, mesh=mesh, in_specs=in_specs, out_specs=out_specs, check_vma=False
    )
```

```python
import functools

import jax
import jax.numpy as jnp
from jax import lax
from jax.experimental import pallas as pl
from jax.experimental.pallas import tpu as pltpu
from jax.sharding import PartitionSpec as P

HIGH_PRECISION = lax.Precision.HIGHEST
adapter_scale = 2.0


def per_device(
    tokens,
    frozen_key_weight,
    adapter_down_maps,
    adapter_up_maps,
    tenant_of_block,
    adapter_of_tenant,
    cotangent,
):
    feats = tokens[0]
    grad_out = cotangent[0]
    owners = tenant_of_block[0]
    slot_table = adapter_of_tenant[0]
    rows = feats.shape[0]
    width = feats.shape[1]
    output_width = frozen_key_weight.shape[1]
    slot_count = adapter_down_maps.shape[1]
    adapter_rank_value = adapter_down_maps.shape[3]
    tenant_ids = jnp.arange(slot_table.shape[0], dtype=jnp.int32)
    slot_block = jnp.sum(
        jnp.where(owners[:, None] == tenant_ids[None, :], slot_table[None, :], 0), axis=1
    )
    slot_row = jnp.repeat(slot_block, rows // owners.shape[0])
    lanes = jnp.arange(slot_count * adapter_rank_value, dtype=jnp.int32) // adapter_rank_value
    slot_selection = (slot_row[:, None] == lanes[None, :]).astype(jnp.float32)
    complete_down_maps = lax.all_gather(adapter_down_maps, "fsdp", axis=2, tiled=True)[0]
    down_flattened = jnp.transpose(complete_down_maps, (1, 0, 2)).reshape(
        width, slot_count * adapter_rank_value
    )
    up_flattened = adapter_up_maps[0].reshape(slot_count * adapter_rank_value, output_width)
    feats32 = feats.astype(jnp.float32)
    low_rank_output = jnp.dot(feats32, down_flattened, precision=HIGH_PRECISION) * slot_selection
    whole_weight = lax.all_gather(frozen_key_weight, "fsdp", axis=0, tiled=True)
    frozen_output = jnp.dot(feats, whole_weight, preferred_element_type=jnp.float32)
    projected = (
        frozen_output
        + adapter_scale * jnp.dot(low_rank_output, up_flattened, precision=HIGH_PRECISION)
    ).astype(jnp.bfloat16)
    gradient_float32 = grad_out.astype(jnp.float32)
    low_rank_gradient = (
        adapter_scale
        * jnp.dot(gradient_float32, up_flattened.T, precision=HIGH_PRECISION)
        * slot_selection
    )
    up_gradient_flattened = adapter_scale * jnp.dot(
        gradient_float32.T, low_rank_output, precision=HIGH_PRECISION
    )
    grad_a_flat = jnp.dot(feats32.T, low_rank_gradient, precision=HIGH_PRECISION)
    back = jnp.dot(grad_out, whole_weight.T, preferred_element_type=jnp.float32)
    token_input_gradient = (
        back + jnp.dot(low_rank_gradient, down_flattened.T, precision=HIGH_PRECISION)
    ).astype(jnp.bfloat16)
    grad_a_local = jnp.transpose(
        grad_a_flat.reshape(width, slot_count, adapter_rank_value), (1, 0, 2)
    )[None]
    grad_b_local = jnp.transpose(
        up_gradient_flattened.reshape(output_width, slot_count, adapter_rank_value), (1, 0, 2)
    )[None]
    down_map_gradient, up_gradient_swapped = (
        lax.psum_scatter(grad_a_local, ("fsdp", "sub"), scatter_dimension=2, tiled=True),
        lax.psum_scatter(grad_b_local, ("fsdp", "sub"), scatter_dimension=2, tiled=True),
    )
    return (projected[None], token_input_gradient[None], down_map_gradient, up_gradient_swapped)


CORES = 2
MESH = pl.DeviceIdType.MESH
bf16, f32 = jnp.bfloat16, jnp.float32


def halves(x):
    high = x.astype(bf16)
    low = (x - high.astype(f32)).astype(bf16)
    return high, low


def dot_nn(a, b):
    return lax.dot_general(a, b, (((1,), (0,)), ((), ())), preferred_element_type=f32)


def dot_nt(a, b):
    return lax.dot_general(a, b, (((1,), (1,)), ((), ())), preferred_element_type=f32)


def pick(z, values):
    out = values[-1]
    for i in range(len(values) - 2, -1, -1):
        out = jnp.where(z == i, values[i], out)
    return out


def step_kernel(
    chips,
    quarters,
    rank,
    tok_in,
    w_ref,
    d_in,
    up_in,
    tenant_in,
    slot_in,
    cot_in,
    proj_ref,
    tg_ref,
    dg_ref,
    ug_ref,
    wbuf,
    dbuf,
    gbuf,
    pbuf,
    rup,
    rdn,
    ubuf,
    urecv,
    dlc,
    acc,
    lacc,
    cw_s,
    cw_r,
    cd_s,
    cd_r,
    sd_s,
    sd_r,
    nb_s,
    nb_r,
    sb_s,
    sb_r,
    so_s,
    so_r,
    pr_s,
    pr_r,
    ch_s,
    up_r,
    dn_r,
    ug_s,
    ug_r,
    cp_s,
    tok_ref,
    d_ref,
    up_ref,
    tenant_ref,
    slot_ref,
    cot_ref,
):
    me = lax.axis_index("fsdp")
    a = lax.axis_index("adapt")
    r = lax.axis_index("rep")
    n = chips * CORES
    z, c = me // CORES, me % CORES
    sib = z * CORES + (1 - c)
    quarter = r * 2 + a
    xq = r * 2 + (1 - a)
    yq = (1 - r) * 2 + a
    dq = (1 - r) * 2 + (1 - a)
    rows, width = tok_in.shape
    depth = width // n
    cols = d_in.shape[0]
    half = wbuf.shape[2] // 2
    upper, lower = z < chips - 1, z > 0
    SIB, XN, YN = {"fsdp": sib}, {"adapt": 1 - a}, {"rep": 1 - r}

    def at(zz, cc=None):
        return zz * CORES + (c if cc is None else cc)

    def rc(src, dst, ss, rs, dev):
        return pltpu.make_async_remote_copy(
            src_ref=src, dst_ref=dst, send_sem=ss, recv_sem=rs, device_id=dev, device_id_type=MESH
        )

    sends = []

    def send(cond, copy):
        if cond is None:
            copy.start()
            sends.append((None, copy))
        else:
            pl.when(cond)(copy.start)
            sends.append((cond, copy))

    def landed(dst, rs):
        rc(dst, dst, sb_s.at[0, 0], rs, SIB).wait_recv()

    fetches = [
        pltpu.make_async_copy(src, dst, cp_s.at[i])
        for i, (src, dst) in enumerate(
            (
                (w_ref, wbuf.at[me]),
                (cot_in, cot_ref),
                (up_in, up_ref),
                (tenant_in, tenant_ref),
                (slot_in, slot_ref),
                (tok_in, tok_ref),
                (d_in, d_ref),
            )
        )
    ]
    for fetch in fetches:
        fetch.start()

    barrier = pltpu.get_barrier_semaphore()
    for i in range(1, n):
        pl.semaphore_signal(barrier, inc=1, device_id={"fsdp": lax.rem(me + i, n)}, device_id_type=MESH)
    pl.semaphore_signal(barrier, inc=1, device_id=XN, device_id_type=MESH)
    pl.semaphore_signal(barrier, inc=1, device_id=YN, device_id_type=MESH)

    fetches[0].wait()
    pl.semaphore_wait(barrier, n - 1 + 2)

    def chain_d(o_z, cond_up, cond_dn):
        ref = dbuf.at[at(o_z)]
        send(cond_up, rc(ref, ref, cd_s.at[0, o_z], cd_r.at[o_z], {"fsdp": at(z + 1)}))
        send(cond_dn, rc(ref, ref, cd_s.at[1, o_z], cd_r.at[o_z], {"fsdp": at(z - 1)}))
        send(None, rc(ref, ref, sd_s.at[o_z], sd_r.at[o_z], SIB))

    def chain_w(o_z, cond_up, cond_dn):
        ref = wbuf.at[at(o_z), quarter]
        send(cond_up, rc(ref, ref, cw_s.at[0, o_z], cw_r.at[o_z], {"fsdp": at(z + 1)}))
        send(cond_dn, rc(ref, ref, cw_s.at[1, o_z], cw_r.at[o_z], {"fsdp": at(z - 1)}))

    chain_w(z, upper, lower)
    whole = wbuf.at[me]
    send(None, rc(whole, whole, so_s, so_r, SIB))

    for fetch in fetches[1:5]:
        fetch.wait()

    owners = tenant_ref.shape[1]
    block = rows // owners
    row_at = lax.broadcasted_iota(jnp.int32, (cols, rows), 1) // block
    want = jnp.zeros((cols, rows), jnp.int32)
    for b in range(owners):
        t = tenant_ref[0, b]
        s = jnp.int32(0)
        for k in range(slot_ref.shape[1]):
            s = s + jnp.where(t == k, slot_ref[0, k], 0)
        want = jnp.where(row_at == b, s, want)
    have = lax.broadcasted_iota(jnp.int32, (cols, rows), 0) // rank
    select = jnp.where(have == want, 2.0, 0.0).astype(f32)
    up_hi, up_lo = halves(up_ref[...])
    cot = cot_ref[...]
    prod = dot_nt(jnp.concatenate([up_hi, up_lo], axis=0), cot)
    dl_hi, dl_lo = halves((prod[:cols] + prod[cols:]) * select)
    dl_hi32, dl_lo32 = dl_hi.astype(f32), dl_lo.astype(f32)
    dlt = jnp.concatenate([dl_hi, dl_lo], axis=0)
    dlc[0] = jnp.concatenate([dl_hi32, dl_lo32], axis=0).T.astype(bf16)
    dlc[1] = jnp.concatenate([dl_lo32, dl_hi32], axis=0).T.astype(bf16)

    for fetch in fetches[5:]:
        fetch.wait()
    d_hi, d_lo = halves(d_ref[...])
    dbuf[me, :cols] = d_hi
    dbuf[me, cols:] = d_lo

    def columns(o):
        return pl.ds(pl.multiple_of(o * depth, depth), depth)

    def grad_chunk(o):
        g = dot_nn(dlt, tok_ref[:, columns(o)])
        gbuf[o] = g[:cols] + g[cols:]

    turn = [pick(z, v) for v in ([3, 3, 0, 0], [2, 0, 3, 1], [1, 2, 1, 2], [0, 1, 2, 3])]
    origin = [pick(z, v) for v in ([1, 0, 3, 2], [2, 2, 1, 1], [3, 3, 0, 0])]

    for t in turn:
        grad_chunk(at(t, 1 - c))
        send(None, rc(gbuf.at[at(t, 1 - c)], pbuf.at[t], pr_s.at[t], pr_r.at[t], SIB))
    for t in turn:
        grad_chunk(at(t))

    def pair_g(t):
        landed(pbuf.at[t], pr_r.at[t])
        gbuf[at(t)] += pbuf[t]

    def gather_g(t):
        @pl.when((t > z) & lower)
        def _():
            landed(rup.at[t], up_r.at[t])
            gbuf[at(t)] += rup[t]

        @pl.when((t < z) & upper)
        def _():
            landed(rdn.at[t], dn_r.at[t])
            gbuf[at(t)] += rdn[t]

    def send_g(t, cond):
        src = gbuf.at[at(t)]
        above, below = (t > z, t < z) if cond is None else (cond & (t > z), cond & (t < z))
        send(above, rc(src, rup.at[t], ch_s.at[t], up_r.at[t], {"fsdp": at(z + 1)}))
        send(below, rc(src, rdn.at[t], ch_s.at[t], dn_r.at[t], {"fsdp": at(z - 1)}))

    def spread_w(o_z):
        ref = wbuf.at[at(o_z), quarter]
        send(None, rc(ref, ref, nb_s.at[0, o_z], nb_r.at[0, o_z], XN))
        send(None, rc(ref, ref, nb_s.at[1, o_z], nb_r.at[1, o_z], YN))
        send(None, rc(ref, ref, sb_s.at[0, o_z], sb_r.at[0, o_z], SIB))

    def swap_w(o_z):
        ref = wbuf.at[at(o_z), xq]
        landed(ref, nb_r.at[0, o_z])
        part = wbuf.at[at(o_z), xq, pl.ds(0, half)]
        send(None, rc(part, part, nb_s.at[2, o_z], nb_r.at[2, o_z], YN))
        send(None, rc(ref, ref, sb_s.at[1, o_z], sb_r.at[1, o_z], SIB))
        ref2 = wbuf.at[at(o_z), yq]
        landed(ref2, nb_r.at[1, o_z])
        part2 = wbuf.at[at(o_z), yq, pl.ds(half, half)]
        send(None, rc(part2, part2, nb_s.at[3, o_z], nb_r.at[3, o_z], XN))
        send(None, rc(ref2, ref2, sb_s.at[2, o_z], sb_r.at[2, o_z], SIB))

    def last_w(o_z):
        landed(wbuf.at[at(o_z), dq, pl.ds(0, half)], nb_r.at[2, o_z])
        landed(wbuf.at[at(o_z), dq, pl.ds(half, half)], nb_r.at[3, o_z])
        ref = wbuf.at[at(o_z), dq]
        send(None, rc(ref, ref, sb_s.at[3, o_z], sb_r.at[3, o_z], SIB))

    def take_w(j):
        o_z = origin[j]
        landed(wbuf.at[at(o_z), quarter], cw_r.at[o_z])
        chain_w(o_z, (o_z < z) & upper, (o_z > z) & lower)
        spread_w(o_z)

    def take_d(j):
        o_z = origin[j]
        landed(dbuf.at[at(o_z)], cd_r.at[o_z])
        chain_d(o_z, (o_z < z) & upper, (o_z > z) & lower)

    ends = (z == 0) | (z == chips - 1)
    take_w(0)
    pair_g(turn[0])
    send_g(turn[0], ends)
    take_w(1)
    chain_d(z, upper, lower)
    swap_w(origin[0])
    take_w(2)
    gather_g(turn[0])
    send_g(turn[0], jnp.logical_not(ends))
    swap_w(origin[1])
    take_d(0)
    pair_g(turn[1])
    gather_g(turn[1])
    send_g(turn[1], None)
    swap_w(origin[2])
    take_d(1)
    pair_g(turn[2])
    gather_g(turn[2])
    send_g(turn[2], None)
    for j in range(chips - 1):
        last_w(origin[j])
    take_d(2)

    for zz in range(chips):
        landed(dbuf.at[at(zz, 1 - c)], sd_r.at[zz])
    lacc[...] = jnp.zeros_like(lacc)

    @pl.loop(0, n)
    def _(o):
        lacc[...] += dot_nt(dbuf[o], tok_ref[:, columns(o)])

    low_hi, low_lo = halves((lacc[:cols] + lacc[cols:]) * select)
    lowc = jnp.concatenate([low_hi.astype(f32), low_lo.astype(f32)], axis=0).T.astype(bf16)
    cot_t = cot.astype(f32).T.astype(bf16)
    share = ubuf.shape[1]
    for f in range(n):
        ubuf[f] = dot_nn(cot_t[f * share : (f + 1) * share], lowc)
    for i in range(1, n):
        f = lax.rem(me + i, n)
        send(None, rc(ubuf.at[f], urecv.at[i], ug_s.at[i], ug_r.at[i], {"fsdp": f}))
    acc[...] = dot_nn(lowc, jnp.concatenate([up_hi, up_hi], axis=0)) + dot_nn(
        lowc, jnp.concatenate([up_lo, up_lo], axis=0)
    )

    def apply_w(o):
        w = wbuf[o].reshape(depth, wbuf.shape[3])
        acc[...] += dot_nn(tok_ref[:, columns(o)], w)
        d2 = dbuf[o]
        back = dot_nt(cot, w) + (dot_nn(dlc[0], d2) + dot_nn(dlc[1], d2))
        tg_ref[:, columns(o)] = back.astype(bf16)

    apply_w(me)
    landed(wbuf.at[sib], so_r)
    apply_w(sib)

    for j in range(chips - 1):
        o_z = origin[j]
        apply_w(at(o_z))
        for k, q in enumerate((quarter, xq, yq, dq)):
            landed(wbuf.at[at(o_z, 1 - c), q], sb_r.at[k, o_z])
        apply_w(at(o_z, 1 - c))

    landed(pbuf.at[z], pr_r.at[z])
    dg_ref[...] = gbuf[me] + pbuf[z]

    @pl.when(lower)
    def _():
        landed(rup.at[z], up_r.at[z])
        dg_ref[...] += rup[z]

    @pl.when(upper)
    def _():
        landed(rdn.at[z], dn_r.at[z])
        dg_ref[...] += rdn[z]

    total = ubuf[me]
    for i in range(1, n):
        landed(urecv.at[i], ug_r.at[i])
        total = total + urecv[i]
    total = total.T
    ug_ref[...] = total[:cols] + total[cols:]
    proj_ref[...] = acc[...].astype(bf16)

    for cond, copy in sends:
        if cond is None:
            copy.wait_send()
        else:
            pl.when(cond)(copy.wait_send)


PIECES = 8


def write_kernel(*refs):
    ins, outs, held, sems = refs[:4], refs[4:8], refs[8:12], refs[12]
    ways = []
    for i in range(4):
        rows = ins[i].shape[0]
        pieces = PIECES if i == 1 else 1
        size = rows // pieces
        for p in range(pieces):
            part = pl.ds(p * size, size)
            k = len(ways)
            ways.append(
                (
                    pltpu.make_async_copy(ins[i].at[part], held[i].at[part], sems.at[0, k]),
                    pltpu.make_async_copy(held[i].at[part], outs[i].at[part], sems.at[1, k]),
                )
            )
    for way in ways:
        way[0].start()
    for way in ways:
        way[0].wait()
        way[1].start()
    for way in ways:
        way[1].wait()


def fused_step(chips, tokens, weight, downs, ups, tenants, slots, cotangent):
    rows, width = tokens.shape[1:]
    depth, out_width = weight.shape
    slot_count, rank = downs.shape[1], downs.shape[3]
    cols = slot_count * rank
    n = chips * CORES
    quarters = 4
    share = out_width // n
    down_t = jnp.transpose(downs[0], (0, 2, 1)).reshape(cols, depth)
    dma = pltpu.SemaphoreType.DMA
    vmem = pl.BlockSpec(memory_space=pltpu.VMEM)
    hbm = pl.BlockSpec(memory_space=pltpu.HBM)
    proj, tg, dg, ug = pl.pallas_call(
        functools.partial(step_kernel, chips, quarters, rank),
        out_shape=(
            jax.ShapeDtypeStruct((rows, out_width), bf16),
            jax.ShapeDtypeStruct((rows, width), bf16),
            jax.ShapeDtypeStruct((cols, depth), f32),
            jax.ShapeDtypeStruct((cols, share), f32),
        ),
        in_specs=[hbm] * 7,
        out_specs=(vmem,) * 4,
        scratch_shapes=[
            pltpu.VMEM((n, quarters, depth // quarters, out_width), bf16),
            pltpu.VMEM((n, 2 * cols, depth), bf16),
            pltpu.VMEM((n, cols, depth), f32),
            pltpu.VMEM((chips, cols, depth), f32),
            pltpu.VMEM((chips, cols, depth), f32),
            pltpu.VMEM((chips, cols, depth), f32),
            pltpu.VMEM((n, share, 2 * cols), f32),
            pltpu.VMEM((n, share, 2 * cols), f32),
            pltpu.VMEM((2, rows, 2 * cols), bf16),
            pltpu.VMEM((rows, out_width), f32),
            pltpu.VMEM((2 * cols, rows), f32),
            dma((2, chips)),
            dma((chips,)),
            dma((2, chips)),
            dma((chips,)),
            dma((chips,)),
            dma((chips,)),
            dma((4, chips)),
            dma((4, chips)),
            dma((4, chips)),
            dma((4, chips)),
            dma,
            dma,
            dma((chips,)),
            dma((chips,)),
            dma((chips,)),
            dma((chips,)),
            dma((chips,)),
            dma((n,)),
            dma((n,)),
            dma((7,)),
            pltpu.VMEM((rows, width), bf16),
            pltpu.VMEM((cols, depth), f32),
            pltpu.VMEM((cols, out_width), f32),
            pltpu.SMEM(tenants.shape, jnp.int32),
            pltpu.SMEM(slots.shape, jnp.int32),
            pltpu.VMEM((rows, out_width), bf16),
        ],
        compiler_params=pltpu.CompilerParams(
            collective_id=0, has_side_effects=True, vmem_limit_bytes=63 * 1024 * 1024
        ),
        cost_estimate=pl.CostEstimate(
            flops=5 * rows * width * out_width, bytes_accessed=8 * 1024 * 1024, transcendentals=0
        ),
    )(
        tokens[0],
        weight.reshape(quarters, depth // quarters, out_width),
        down_t,
        ups[0].reshape(cols, out_width),
        tenants,
        slots,
        cotangent[0],
    )
    proj, tg, dg, ug = pl.pallas_call(
        write_kernel,
        out_shape=tuple(jax.ShapeDtypeStruct(x.shape, x.dtype) for x in (proj, tg, dg, ug)),
        in_specs=[pl.BlockSpec(memory_space=pl.ANY)] * 4,
        out_specs=(hbm,) * 4,
        scratch_shapes=[pltpu.VMEM(x.shape, x.dtype) for x in (proj, tg, dg, ug)]
        + [dma((2, PIECES + 3))],
        compiler_params=pltpu.CompilerParams(vmem_limit_bytes=63 * 1024 * 1024),
        cost_estimate=pl.CostEstimate(flops=0, bytes_accessed=4 * rows * width, transcendentals=0),
    )(proj, tg, dg, ug)
    down_gradient = jnp.transpose(dg.reshape(slot_count, rank, depth), (0, 2, 1))[None]
    up_gradient = jnp.transpose(ug.reshape(slot_count, rank, share), (0, 2, 1))[None]
    return proj[None], tg[None], down_gradient, up_gradient


def solution(mesh):
    sizes = (mesh.shape["rep"], mesh.shape["fsdp"], mesh.shape["adapt"], mesh.shape["sub"])
    body = functools.partial(fused_step, sizes[1] // CORES) if sizes == (2, 8, 2, 1) else per_device
    in_specs = (
        P("adapt", ("rep", "fsdp", "sub"), None),
        P("fsdp", None),
        P("adapt", "rep", "fsdp", None),
        P("adapt", "rep", None, None),
        P("adapt", ("rep", "fsdp", "sub")),
        P("adapt", "rep"),
        P("adapt", ("rep", "fsdp", "sub"), None),
    )
    out_specs = (
        P("adapt", ("rep", "fsdp", "sub"), None),
        P("adapt", ("rep", "fsdp", "sub"), None),
        P("adapt", "rep", ("fsdp", "sub"), None),
        P("adapt", "rep", ("fsdp", "sub"), None),
    )
    return jax.shard_map(
        body, mesh=mesh, in_specs=in_specs, out_specs=out_specs, check_vma=False
    )
```

```python
import functools

import jax
import jax.numpy as jnp
from jax import lax
from jax.experimental import pallas as pl
from jax.experimental.pallas import tpu as pltpu
from jax.sharding import PartitionSpec as P

HIGH_PRECISION = lax.Precision.HIGHEST
adapter_scale = 2.0


def per_device(
    tokens,
    frozen_key_weight,
    adapter_down_maps,
    adapter_up_maps,
    tenant_of_block,
    adapter_of_tenant,
    cotangent,
):
    feats = tokens[0]
    grad_out = cotangent[0]
    owners = tenant_of_block[0]
    slot_table = adapter_of_tenant[0]
    rows = feats.shape[0]
    width = feats.shape[1]
    output_width = frozen_key_weight.shape[1]
    slot_count = adapter_down_maps.shape[1]
    adapter_rank_value = adapter_down_maps.shape[3]
    tenant_ids = jnp.arange(slot_table.shape[0], dtype=jnp.int32)
    slot_block = jnp.sum(
        jnp.where(owners[:, None] == tenant_ids[None, :], slot_table[None, :], 0), axis=1
    )
    slot_row = jnp.repeat(slot_block, rows // owners.shape[0])
    lanes = jnp.arange(slot_count * adapter_rank_value, dtype=jnp.int32) // adapter_rank_value
    slot_selection = (slot_row[:, None] == lanes[None, :]).astype(jnp.float32)
    complete_down_maps = lax.all_gather(adapter_down_maps, "fsdp", axis=2, tiled=True)[0]
    down_flattened = jnp.transpose(complete_down_maps, (1, 0, 2)).reshape(
        width, slot_count * adapter_rank_value
    )
    up_flattened = adapter_up_maps[0].reshape(slot_count * adapter_rank_value, output_width)
    feats32 = feats.astype(jnp.float32)
    low_rank_output = jnp.dot(feats32, down_flattened, precision=HIGH_PRECISION) * slot_selection
    whole_weight = lax.all_gather(frozen_key_weight, "fsdp", axis=0, tiled=True)
    frozen_output = jnp.dot(feats, whole_weight, preferred_element_type=jnp.float32)
    projected = (
        frozen_output
        + adapter_scale * jnp.dot(low_rank_output, up_flattened, precision=HIGH_PRECISION)
    ).astype(jnp.bfloat16)
    gradient_float32 = grad_out.astype(jnp.float32)
    low_rank_gradient = (
        adapter_scale
        * jnp.dot(gradient_float32, up_flattened.T, precision=HIGH_PRECISION)
        * slot_selection
    )
    up_gradient_flattened = adapter_scale * jnp.dot(
        gradient_float32.T, low_rank_output, precision=HIGH_PRECISION
    )
    grad_a_flat = jnp.dot(feats32.T, low_rank_gradient, precision=HIGH_PRECISION)
    back = jnp.dot(grad_out, whole_weight.T, preferred_element_type=jnp.float32)
    token_input_gradient = (
        back + jnp.dot(low_rank_gradient, down_flattened.T, precision=HIGH_PRECISION)
    ).astype(jnp.bfloat16)
    grad_a_local = jnp.transpose(
        grad_a_flat.reshape(width, slot_count, adapter_rank_value), (1, 0, 2)
    )[None]
    grad_b_local = jnp.transpose(
        up_gradient_flattened.reshape(output_width, slot_count, adapter_rank_value), (1, 0, 2)
    )[None]
    down_map_gradient, up_gradient_swapped = (
        lax.psum_scatter(grad_a_local, ("fsdp", "sub"), scatter_dimension=2, tiled=True),
        lax.psum_scatter(grad_b_local, ("fsdp", "sub"), scatter_dimension=2, tiled=True),
    )
    return (projected[None], token_input_gradient[None], down_map_gradient, up_gradient_swapped)


CORES = 2
MESH = pl.DeviceIdType.MESH
bf16, f32 = jnp.bfloat16, jnp.float32


def halves(x):
    high = x.astype(bf16)
    low = (x - high.astype(f32)).astype(bf16)
    return high, low


def dot_nn(a, b):
    return lax.dot_general(a, b, (((1,), (0,)), ((), ())), preferred_element_type=f32)


def dot_nt(a, b):
    return lax.dot_general(a, b, (((1,), (1,)), ((), ())), preferred_element_type=f32)


def pick(z, values):
    out = values[-1]
    for i in range(len(values) - 2, -1, -1):
        out = jnp.where(z == i, values[i], out)
    return out


def step_kernel(
    chips,
    quarters,
    rank,
    tok_in,
    w_ref,
    d_in,
    up_in,
    tenant_in,
    slot_in,
    cot_in,
    proj_ref,
    tg_out,
    dg_ref,
    ug_ref,
    wbuf,
    dbuf,
    gbuf,
    pbuf,
    rup,
    rdn,
    ubuf,
    urecv,
    dlc,
    acc,
    lacc,
    cw_s,
    cw_r,
    cd_s,
    cd_r,
    sd_s,
    sd_r,
    nb_s,
    nb_r,
    sb_s,
    sb_r,
    so_s,
    so_r,
    pr_s,
    pr_r,
    ch_s,
    up_r,
    dn_r,
    ug_s,
    ug_r,
    cp_s,
    tok_ref,
    d_ref,
    up_ref,
    tenant_ref,
    slot_ref,
    cot_ref,
    tgf,
    tg_ref,
    tg_s,
):
    me = lax.axis_index("fsdp")
    a = lax.axis_index("adapt")
    r = lax.axis_index("rep")
    n = chips * CORES
    z, c = me // CORES, me % CORES
    sib = z * CORES + (1 - c)
    quarter = r * 2 + a
    xq = r * 2 + (1 - a)
    yq = (1 - r) * 2 + a
    dq = (1 - r) * 2 + (1 - a)
    rows, width = tok_in.shape
    depth = width // n
    cols = d_in.shape[0]
    half = wbuf.shape[2] // 2
    upper, lower = z < chips - 1, z > 0
    SIB, XN, YN = {"fsdp": sib}, {"adapt": 1 - a}, {"rep": 1 - r}

    def at(zz, cc=None):
        return zz * CORES + (c if cc is None else cc)

    def rc(src, dst, ss, rs, dev):
        return pltpu.make_async_remote_copy(
            src_ref=src, dst_ref=dst, send_sem=ss, recv_sem=rs, device_id=dev, device_id_type=MESH
        )

    sends = []

    def send(cond, copy):
        if cond is None:
            copy.start()
            sends.append((None, copy))
        else:
            pl.when(cond)(copy.start)
            sends.append((cond, copy))

    def landed(dst, rs):
        rc(dst, dst, sb_s.at[0, 0], rs, SIB).wait_recv()

    fetches = [
        pltpu.make_async_copy(src, dst, cp_s.at[i])
        for i, (src, dst) in enumerate(
            (
                (w_ref, wbuf.at[me]),
                (cot_in, cot_ref),
                (up_in, up_ref),
                (tenant_in, tenant_ref),
                (slot_in, slot_ref),
                (tok_in, tok_ref),
                (d_in, d_ref),
            )
        )
    ]
    for fetch in fetches:
        fetch.start()

    barrier = pltpu.get_barrier_semaphore()
    for i in range(1, n):
        pl.semaphore_signal(barrier, inc=1, device_id={"fsdp": lax.rem(me + i, n)}, device_id_type=MESH)
    pl.semaphore_signal(barrier, inc=1, device_id=XN, device_id_type=MESH)
    pl.semaphore_signal(barrier, inc=1, device_id=YN, device_id_type=MESH)

    fetches[0].wait()
    pl.semaphore_wait(barrier, n - 1 + 2)

    def chain_d(o_z, cond_up, cond_dn):
        ref = dbuf.at[at(o_z)]
        send(cond_up, rc(ref, ref, cd_s.at[0, o_z], cd_r.at[o_z], {"fsdp": at(z + 1)}))
        send(cond_dn, rc(ref, ref, cd_s.at[1, o_z], cd_r.at[o_z], {"fsdp": at(z - 1)}))
        send(None, rc(ref, ref, sd_s.at[o_z], sd_r.at[o_z], SIB))

    def chain_w(o_z, cond_up, cond_dn):
        ref = wbuf.at[at(o_z), quarter]
        send(cond_up, rc(ref, ref, cw_s.at[0, o_z], cw_r.at[o_z], {"fsdp": at(z + 1)}))
        send(cond_dn, rc(ref, ref, cw_s.at[1, o_z], cw_r.at[o_z], {"fsdp": at(z - 1)}))

    chain_w(z, upper, lower)
    whole = wbuf.at[me]
    send(None, rc(whole, whole, so_s, so_r, SIB))

    for fetch in fetches[1:5]:
        fetch.wait()

    owners = tenant_ref.shape[1]
    block = rows // owners
    row_at = lax.broadcasted_iota(jnp.int32, (cols, rows), 1) // block
    want = jnp.zeros((cols, rows), jnp.int32)
    for b in range(owners):
        t = tenant_ref[0, b]
        s = jnp.int32(0)
        for k in range(slot_ref.shape[1]):
            s = s + jnp.where(t == k, slot_ref[0, k], 0)
        want = jnp.where(row_at == b, s, want)
    have = lax.broadcasted_iota(jnp.int32, (cols, rows), 0) // rank
    select = jnp.where(have == want, 2.0, 0.0).astype(f32)
    up_hi, up_lo = halves(up_ref[...])
    cot = cot_ref[...]
    prod = dot_nt(jnp.concatenate([up_hi, up_lo], axis=0), cot)
    dl_hi, dl_lo = halves((prod[:cols] + prod[cols:]) * select)
    dl_hi32, dl_lo32 = dl_hi.astype(f32), dl_lo.astype(f32)
    dlt = jnp.concatenate([dl_hi, dl_lo], axis=0)
    dlc[0] = jnp.concatenate([dl_hi32, dl_lo32], axis=0).T.astype(bf16)
    dlc[1] = jnp.concatenate([dl_lo32, dl_hi32], axis=0).T.astype(bf16)

    for fetch in fetches[5:]:
        fetch.wait()
    d_hi, d_lo = halves(d_ref[...])
    dbuf[me, :cols] = d_hi
    dbuf[me, cols:] = d_lo

    def columns(o):
        return pl.ds(pl.multiple_of(o * depth, depth), depth)

    def grad_chunk(o):
        g = dot_nn(dlt, tok_ref[:, columns(o)])
        gbuf[o] = g[:cols] + g[cols:]

    turn = [pick(z, v) for v in ([3, 3, 0, 0], [2, 0, 3, 1], [1, 2, 1, 2], [0, 1, 2, 3])]
    origin = [pick(z, v) for v in ([1, 0, 3, 2], [2, 2, 1, 1], [3, 3, 0, 0])]

    for t in turn:
        grad_chunk(at(t, 1 - c))
        send(None, rc(gbuf.at[at(t, 1 - c)], pbuf.at[t], pr_s.at[t], pr_r.at[t], SIB))
    chain_d(z, upper, lower)
    for t in turn:
        grad_chunk(at(t))

    def pair_g(t):
        landed(pbuf.at[t], pr_r.at[t])
        gbuf[at(t)] += pbuf[t]

    def gather_g(t):
        @pl.when((t > z) & lower)
        def _():
            landed(rup.at[t], up_r.at[t])
            gbuf[at(t)] += rup[t]

        @pl.when((t < z) & upper)
        def _():
            landed(rdn.at[t], dn_r.at[t])
            gbuf[at(t)] += rdn[t]

    def send_g(t, cond):
        src = gbuf.at[at(t)]
        above, below = (t > z, t < z) if cond is None else (cond & (t > z), cond & (t < z))
        send(above, rc(src, rup.at[t], ch_s.at[t], up_r.at[t], {"fsdp": at(z + 1)}))
        send(below, rc(src, rdn.at[t], ch_s.at[t], dn_r.at[t], {"fsdp": at(z - 1)}))

    def spread_w(o_z):
        ref = wbuf.at[at(o_z), quarter]
        send(None, rc(ref, ref, nb_s.at[0, o_z], nb_r.at[0, o_z], XN))
        send(None, rc(ref, ref, nb_s.at[1, o_z], nb_r.at[1, o_z], YN))
        send(None, rc(ref, ref, sb_s.at[0, o_z], sb_r.at[0, o_z], SIB))

    def swap_w(o_z):
        ref = wbuf.at[at(o_z), xq]
        landed(ref, nb_r.at[0, o_z])
        part = wbuf.at[at(o_z), xq, pl.ds(0, half)]
        send(None, rc(part, part, nb_s.at[2, o_z], nb_r.at[2, o_z], YN))
        send(None, rc(ref, ref, sb_s.at[1, o_z], sb_r.at[1, o_z], SIB))
        ref2 = wbuf.at[at(o_z), yq]
        landed(ref2, nb_r.at[1, o_z])
        part2 = wbuf.at[at(o_z), yq, pl.ds(half, half)]
        send(None, rc(part2, part2, nb_s.at[3, o_z], nb_r.at[3, o_z], XN))
        send(None, rc(ref2, ref2, sb_s.at[2, o_z], sb_r.at[2, o_z], SIB))

    def last_w(o_z):
        landed(wbuf.at[at(o_z), dq, pl.ds(0, half)], nb_r.at[2, o_z])
        landed(wbuf.at[at(o_z), dq, pl.ds(half, half)], nb_r.at[3, o_z])
        ref = wbuf.at[at(o_z), dq]
        send(None, rc(ref, ref, sb_s.at[3, o_z], sb_r.at[3, o_z], SIB))

    def take_w(j):
        o_z = origin[j]
        landed(wbuf.at[at(o_z), quarter], cw_r.at[o_z])
        chain_w(o_z, (o_z < z) & upper, (o_z > z) & lower)
        spread_w(o_z)

    def take_d(j):
        o_z = origin[j]
        landed(dbuf.at[at(o_z)], cd_r.at[o_z])
        chain_d(o_z, (o_z < z) & upper, (o_z > z) & lower)

    def base_w(o):
        w = wbuf[o].reshape(depth, wbuf.shape[3])
        acc[...] += dot_nn(tok_ref[:, columns(o)], w)
        tgf[:, columns(o)] = dot_nt(cot_ref[...], w)

    def low_d(o):
        lacc[...] += dot_nt(dbuf[o], tok_ref[:, columns(o)])

    def tg_copy(o):
        return pltpu.make_async_copy(tg_ref.at[:, columns(o)], tg_out.at[:, columns(o)], tg_s.at[o])

    def back_d(o):
        d2 = dbuf[o]
        back = tgf[:, columns(o)] + (dot_nn(dlc[0], d2) + dot_nn(dlc[1], d2))
        tg_ref[:, columns(o)] = back.astype(bf16)
        tg_copy(o).start()

    ends = (z == 0) | (z == chips - 1)
    inner = jnp.logical_not(ends)
    acc[...] = jnp.zeros_like(acc)
    lacc[...] = jnp.zeros_like(lacc)
    take_w(0)
    pair_g(turn[0])
    send_g(turn[0], ends)
    take_w(1)
    base_w(me)
    swap_w(origin[0])
    take_w(2)
    gather_g(turn[0])
    send_g(turn[0], inner)
    low_d(me)
    swap_w(origin[1])
    take_d(0)
    low_d(at(origin[0]))
    landed(wbuf.at[sib], so_r)
    base_w(sib)
    pair_g(turn[1])
    gather_g(turn[1])
    send_g(turn[1], None)
    swap_w(origin[2])
    take_d(1)
    low_d(at(origin[1]))
    pair_g(turn[2])
    send_g(turn[2], ends)
    last_w(origin[0])
    base_w(at(origin[0]))
    last_w(origin[1])
    take_d(2)
    gather_g(turn[2])
    send_g(turn[2], inner)
    base_w(at(origin[1]))
    low_d(at(origin[2]))
    for zz in [z] + origin:
        landed(dbuf.at[at(zz, 1 - c)], sd_r.at[zz])
        low_d(at(zz, 1 - c))

    low_hi, low_lo = halves((lacc[:cols] + lacc[cols:]) * select)
    lowc = jnp.concatenate([low_hi.astype(f32), low_lo.astype(f32)], axis=0).T.astype(bf16)
    cot_t = cot.astype(f32).T.astype(bf16)
    share = ubuf.shape[1]
    for f in range(n):
        ubuf[f] = dot_nn(cot_t[f * share : (f + 1) * share], lowc)
    for i in range(1, n):
        f = lax.rem(me + i, n)
        send(None, rc(ubuf.at[f], urecv.at[i], ug_s.at[i], ug_r.at[i], {"fsdp": f}))
    last_w(origin[2])
    acc[...] += dot_nn(lowc, jnp.concatenate([up_hi, up_hi], axis=0)) + dot_nn(
        lowc, jnp.concatenate([up_lo, up_lo], axis=0)
    )
    for o in (me, sib, at(origin[0]), at(origin[1])):
        back_d(o)
    base_w(at(origin[2]))
    back_d(at(origin[2]))
    for o_z in origin:
        for k, q in enumerate((quarter, xq, yq, dq)):
            landed(wbuf.at[at(o_z, 1 - c), q], sb_r.at[k, o_z])
        base_w(at(o_z, 1 - c))
        back_d(at(o_z, 1 - c))

    landed(pbuf.at[z], pr_r.at[z])
    dg_ref[...] = gbuf[me] + pbuf[z]

    @pl.when(lower)
    def _():
        landed(rup.at[z], up_r.at[z])
        dg_ref[...] += rup[z]

    @pl.when(upper)
    def _():
        landed(rdn.at[z], dn_r.at[z])
        dg_ref[...] += rdn[z]

    total = ubuf[me]
    for i in range(1, n):
        landed(urecv.at[i], ug_r.at[i])
        total = total + urecv[i]
    total = total.T
    ug_ref[...] = total[:cols] + total[cols:]
    proj_ref[...] = acc[...].astype(bf16)

    for o in range(n):
        tg_copy(o).wait()
    for cond, copy in sends:
        if cond is None:
            copy.wait_send()
        else:
            pl.when(cond)(copy.wait_send)


PIECES = 8


def write_kernel(*refs):
    ins, outs, held, sems = refs[:4], refs[4:8], refs[8:12], refs[12]
    ways = []
    for i in range(4):
        rows = ins[i].shape[0]
        pieces = PIECES if i == 1 else 1
        size = rows // pieces
        for p in range(pieces):
            part = pl.ds(p * size, size)
            k = len(ways)
            ways.append(
                (
                    pltpu.make_async_copy(ins[i].at[part], held[i].at[part], sems.at[0, k]),
                    pltpu.make_async_copy(held[i].at[part], outs[i].at[part], sems.at[1, k]),
                )
            )
    for way in ways:
        way[0].start()
    for way in ways:
        way[0].wait()
        way[1].start()
    for way in ways:
        way[1].wait()


def fused_step(chips, tokens, weight, downs, ups, tenants, slots, cotangent):
    rows, width = tokens.shape[1:]
    depth, out_width = weight.shape
    slot_count, rank = downs.shape[1], downs.shape[3]
    cols = slot_count * rank
    n = chips * CORES
    quarters = 4
    share = out_width // n
    down_t = jnp.transpose(downs[0], (0, 2, 1)).reshape(cols, depth)
    dma = pltpu.SemaphoreType.DMA
    vmem = pl.BlockSpec(memory_space=pltpu.VMEM)
    hbm = pl.BlockSpec(memory_space=pltpu.HBM)
    proj, tg, dg, ug = pl.pallas_call(
        functools.partial(step_kernel, chips, quarters, rank),
        out_shape=(
            jax.ShapeDtypeStruct((rows, out_width), bf16),
            jax.ShapeDtypeStruct((rows, width), bf16),
            jax.ShapeDtypeStruct((cols, depth), f32),
            jax.ShapeDtypeStruct((cols, share), f32),
        ),
        in_specs=[hbm] * 7,
        out_specs=(vmem, hbm, vmem, vmem),
        scratch_shapes=[
            pltpu.VMEM((n, quarters, depth // quarters, out_width), bf16),
            pltpu.VMEM((n, 2 * cols, depth), bf16),
            pltpu.VMEM((n, cols, depth), f32),
            pltpu.VMEM((chips, cols, depth), f32),
            pltpu.VMEM((chips, cols, depth), f32),
            pltpu.VMEM((chips, cols, depth), f32),
            pltpu.VMEM((n, share, 2 * cols), f32),
            pltpu.VMEM((n, share, 2 * cols), f32),
            pltpu.VMEM((2, rows, 2 * cols), bf16),
            pltpu.VMEM((rows, out_width), f32),
            pltpu.VMEM((2 * cols, rows), f32),
            dma((2, chips)),
            dma((chips,)),
            dma((2, chips)),
            dma((chips,)),
            dma((chips,)),
            dma((chips,)),
            dma((4, chips)),
            dma((4, chips)),
            dma((4, chips)),
            dma((4, chips)),
            dma,
            dma,
            dma((chips,)),
            dma((chips,)),
            dma((chips,)),
            dma((chips,)),
            dma((chips,)),
            dma((n,)),
            dma((n,)),
            dma((7,)),
            pltpu.VMEM((rows, width), bf16),
            pltpu.VMEM((cols, depth), f32),
            pltpu.VMEM((cols, out_width), f32),
            pltpu.SMEM(tenants.shape, jnp.int32),
            pltpu.SMEM(slots.shape, jnp.int32),
            pltpu.VMEM((rows, out_width), bf16),
            pltpu.VMEM((rows, width), f32),
            pltpu.VMEM((rows, width), bf16),
            dma((n,)),
        ],
        compiler_params=pltpu.CompilerParams(
            collective_id=0, has_side_effects=True, vmem_limit_bytes=63 * 1024 * 1024
        ),
        cost_estimate=pl.CostEstimate(
            flops=5 * rows * width * out_width, bytes_accessed=8 * 1024 * 1024, transcendentals=0
        ),
    )(
        tokens[0],
        weight.reshape(quarters, depth // quarters, out_width),
        down_t,
        ups[0].reshape(cols, out_width),
        tenants,
        slots,
        cotangent[0],
    )
    proj, tg, dg, ug = pl.pallas_call(
        write_kernel,
        out_shape=tuple(jax.ShapeDtypeStruct(x.shape, x.dtype) for x in (proj, tg, dg, ug)),
        in_specs=[pl.BlockSpec(memory_space=pl.ANY)] * 4,
        out_specs=(hbm,) * 4,
        scratch_shapes=[pltpu.VMEM(x.shape, x.dtype) for x in (proj, tg, dg, ug)]
        + [dma((2, PIECES + 3))],
        compiler_params=pltpu.CompilerParams(vmem_limit_bytes=63 * 1024 * 1024),
        cost_estimate=pl.CostEstimate(flops=0, bytes_accessed=4 * rows * width, transcendentals=0),
    )(proj, tg, dg, ug)
    down_gradient = jnp.transpose(dg.reshape(slot_count, rank, depth), (0, 2, 1))[None]
    up_gradient = jnp.transpose(ug.reshape(slot_count, rank, share), (0, 2, 1))[None]
    return proj[None], tg[None], down_gradient, up_gradient


def solution(mesh):
    sizes = (mesh.shape["rep"], mesh.shape["fsdp"], mesh.shape["adapt"], mesh.shape["sub"])
    body = functools.partial(fused_step, sizes[1] // CORES) if sizes == (2, 8, 2, 1) else per_device
    in_specs = (
        P("adapt", ("rep", "fsdp", "sub"), None),
        P("fsdp", None),
        P("adapt", "rep", "fsdp", None),
        P("adapt", "rep", None, None),
        P("adapt", ("rep", "fsdp", "sub")),
        P("adapt", "rep"),
        P("adapt", ("rep", "fsdp", "sub"), None),
    )
    out_specs = (
        P("adapt", ("rep", "fsdp", "sub"), None),
        P("adapt", ("rep", "fsdp", "sub"), None),
        P("adapt", "rep", ("fsdp", "sub"), None),
        P("adapt", "rep", ("fsdp", "sub"), None),
    )
    return jax.shard_map(
        body, mesh=mesh, in_specs=in_specs, out_specs=out_specs, check_vma=False
    )
```

```python
import functools

import jax
import jax.numpy as jnp
from jax import lax
from jax.experimental import pallas as pl
from jax.experimental.pallas import tpu as pltpu
from jax.sharding import PartitionSpec as P

HIGH_PRECISION = lax.Precision.HIGHEST
adapter_scale = 2.0


def per_device(
    tokens,
    frozen_key_weight,
    adapter_down_maps,
    adapter_up_maps,
    tenant_of_block,
    adapter_of_tenant,
    cotangent,
):
    feats = tokens[0]
    grad_out = cotangent[0]
    owners = tenant_of_block[0]
    slot_table = adapter_of_tenant[0]
    rows = feats.shape[0]
    width = feats.shape[1]
    output_width = frozen_key_weight.shape[1]
    slot_count = adapter_down_maps.shape[1]
    adapter_rank_value = adapter_down_maps.shape[3]
    tenant_ids = jnp.arange(slot_table.shape[0], dtype=jnp.int32)
    slot_block = jnp.sum(
        jnp.where(owners[:, None] == tenant_ids[None, :], slot_table[None, :], 0), axis=1
    )
    slot_row = jnp.repeat(slot_block, rows // owners.shape[0])
    lanes = jnp.arange(slot_count * adapter_rank_value, dtype=jnp.int32) // adapter_rank_value
    slot_selection = (slot_row[:, None] == lanes[None, :]).astype(jnp.float32)
    complete_down_maps = lax.all_gather(adapter_down_maps, "fsdp", axis=2, tiled=True)[0]
    down_flattened = jnp.transpose(complete_down_maps, (1, 0, 2)).reshape(
        width, slot_count * adapter_rank_value
    )
    up_flattened = adapter_up_maps[0].reshape(slot_count * adapter_rank_value, output_width)
    feats32 = feats.astype(jnp.float32)
    low_rank_output = jnp.dot(feats32, down_flattened, precision=HIGH_PRECISION) * slot_selection
    whole_weight = lax.all_gather(frozen_key_weight, "fsdp", axis=0, tiled=True)
    frozen_output = jnp.dot(feats, whole_weight, preferred_element_type=jnp.float32)
    projected = (
        frozen_output
        + adapter_scale * jnp.dot(low_rank_output, up_flattened, precision=HIGH_PRECISION)
    ).astype(jnp.bfloat16)
    gradient_float32 = grad_out.astype(jnp.float32)
    low_rank_gradient = (
        adapter_scale
        * jnp.dot(gradient_float32, up_flattened.T, precision=HIGH_PRECISION)
        * slot_selection
    )
    up_gradient_flattened = adapter_scale * jnp.dot(
        gradient_float32.T, low_rank_output, precision=HIGH_PRECISION
    )
    grad_a_flat = jnp.dot(feats32.T, low_rank_gradient, precision=HIGH_PRECISION)
    back = jnp.dot(grad_out, whole_weight.T, preferred_element_type=jnp.float32)
    token_input_gradient = (
        back + jnp.dot(low_rank_gradient, down_flattened.T, precision=HIGH_PRECISION)
    ).astype(jnp.bfloat16)
    grad_a_local = jnp.transpose(
        grad_a_flat.reshape(width, slot_count, adapter_rank_value), (1, 0, 2)
    )[None]
    grad_b_local = jnp.transpose(
        up_gradient_flattened.reshape(output_width, slot_count, adapter_rank_value), (1, 0, 2)
    )[None]
    down_map_gradient, up_gradient_swapped = (
        lax.psum_scatter(grad_a_local, ("fsdp", "sub"), scatter_dimension=2, tiled=True),
        lax.psum_scatter(grad_b_local, ("fsdp", "sub"), scatter_dimension=2, tiled=True),
    )
    return (projected[None], token_input_gradient[None], down_map_gradient, up_gradient_swapped)


CORES = 2
MESH = pl.DeviceIdType.MESH
bf16, f32 = jnp.bfloat16, jnp.float32


def halves(x):
    high = x.astype(bf16)
    low = (x - high.astype(f32)).astype(bf16)
    return high, low


def dot_nn(a, b):
    return lax.dot_general(a, b, (((1,), (0,)), ((), ())), preferred_element_type=f32)


def dot_nt(a, b):
    return lax.dot_general(a, b, (((1,), (1,)), ((), ())), preferred_element_type=f32)


def pick(z, values):
    out = values[-1]
    for i in range(len(values) - 2, -1, -1):
        out = jnp.where(z == i, values[i], out)
    return out


def step_kernel(
    chips,
    quarters,
    rank,
    tok_in,
    w_ref,
    d_in,
    up_in,
    tenant_in,
    slot_in,
    cot_in,
    proj_ref,
    tg_out,
    dg_ref,
    ug_ref,
    wbuf,
    dbuf,
    gbuf,
    pbuf,
    rup,
    rdn,
    ubuf,
    urecv,
    dlc,
    acc,
    lacc,
    cw_s,
    cw_r,
    cd_s,
    cd_r,
    sd_s,
    sd_r,
    nb_s,
    nb_r,
    sb_s,
    sb_r,
    so_s,
    so_r,
    pr_s,
    pr_r,
    ch_s,
    up_r,
    dn_r,
    ug_s,
    ug_r,
    cp_s,
    tok_ref,
    d_ref,
    up_ref,
    tenant_ref,
    slot_ref,
    cot_ref,
    tgf,
    tg_ref,
    tg_s,
):
    me = lax.axis_index("fsdp")
    a = lax.axis_index("adapt")
    r = lax.axis_index("rep")
    n = chips * CORES
    z, c = me // CORES, me % CORES
    sib = z * CORES + (1 - c)
    quarter = r * 2 + a
    xq = r * 2 + (1 - a)
    yq = (1 - r) * 2 + a
    dq = (1 - r) * 2 + (1 - a)
    rows, width = tok_in.shape
    depth = width // n
    cols = d_in.shape[0]
    half = wbuf.shape[2] // 2
    upper, lower = z < chips - 1, z > 0
    SIB, XN, YN = {"fsdp": sib}, {"adapt": 1 - a}, {"rep": 1 - r}

    def at(zz, cc=None):
        return zz * CORES + (c if cc is None else cc)

    def rc(src, dst, ss, rs, dev):
        return pltpu.make_async_remote_copy(
            src_ref=src, dst_ref=dst, send_sem=ss, recv_sem=rs, device_id=dev, device_id_type=MESH
        )

    sends = []

    def send(cond, copy):
        if cond is None:
            copy.start()
            sends.append((None, copy))
        else:
            pl.when(cond)(copy.start)
            sends.append((cond, copy))

    def landed(dst, rs):
        rc(dst, dst, sb_s.at[0, 0], rs, SIB).wait_recv()

    fetches = [
        pltpu.make_async_copy(src, dst, cp_s.at[i])
        for i, (src, dst) in enumerate(
            (
                (w_ref, wbuf.at[me]),
                (cot_in, cot_ref),
                (up_in, up_ref),
                (tenant_in, tenant_ref),
                (slot_in, slot_ref),
                (tok_in, tok_ref),
                (d_in, d_ref),
            )
        )
    ]
    for fetch in fetches:
        fetch.start()

    barrier = pltpu.get_barrier_semaphore()
    for i in range(1, n):
        pl.semaphore_signal(barrier, inc=1, device_id={"fsdp": lax.rem(me + i, n)}, device_id_type=MESH)
    pl.semaphore_signal(barrier, inc=1, device_id=XN, device_id_type=MESH)
    pl.semaphore_signal(barrier, inc=1, device_id=YN, device_id_type=MESH)

    fetches[0].wait()
    pl.semaphore_wait(barrier, n - 1 + 2)

    def chain_d(o_z, cond_up, cond_dn):
        ref = dbuf.at[at(o_z)]
        send(cond_up, rc(ref, ref, cd_s.at[0, o_z], cd_r.at[o_z], {"fsdp": at(z + 1)}))
        send(cond_dn, rc(ref, ref, cd_s.at[1, o_z], cd_r.at[o_z], {"fsdp": at(z - 1)}))
        send(None, rc(ref, ref, sd_s.at[o_z], sd_r.at[o_z], SIB))

    def chain_w(o_z, cond_up, cond_dn):
        ref = wbuf.at[at(o_z), quarter]
        send(cond_up, rc(ref, ref, cw_s.at[0, o_z], cw_r.at[o_z], {"fsdp": at(z + 1)}))
        send(cond_dn, rc(ref, ref, cw_s.at[1, o_z], cw_r.at[o_z], {"fsdp": at(z - 1)}))

    chain_w(z, upper, lower)
    whole = wbuf.at[me]
    send(None, rc(whole, whole, so_s, so_r, SIB))

    for fetch in fetches[1:5]:
        fetch.wait()

    owners = tenant_ref.shape[1]
    block = rows // owners
    row_at = lax.broadcasted_iota(jnp.int32, (cols, rows), 1) // block
    want = jnp.zeros((cols, rows), jnp.int32)
    for b in range(owners):
        t = tenant_ref[0, b]
        s = jnp.int32(0)
        for k in range(slot_ref.shape[1]):
            s = s + jnp.where(t == k, slot_ref[0, k], 0)
        want = jnp.where(row_at == b, s, want)
    have = lax.broadcasted_iota(jnp.int32, (cols, rows), 0) // rank
    select = jnp.where(have == want, 2.0, 0.0).astype(f32)
    up_hi, up_lo = halves(up_ref[...])
    cot = cot_ref[...]
    prod = dot_nt(jnp.concatenate([up_hi, up_lo], axis=0), cot)
    dl_hi, dl_lo = halves((prod[:cols] + prod[cols:]) * select)
    dl_hi32, dl_lo32 = dl_hi.astype(f32), dl_lo.astype(f32)
    dlt = jnp.concatenate([dl_hi, dl_lo], axis=0)
    dlc[0] = jnp.concatenate([dl_hi32, dl_lo32], axis=0).T.astype(bf16)
    dlc[1] = jnp.concatenate([dl_lo32, dl_hi32], axis=0).T.astype(bf16)

    for fetch in fetches[5:]:
        fetch.wait()
    d_hi, d_lo = halves(d_ref[...])
    dbuf[me, :cols] = d_hi
    dbuf[me, cols:] = d_lo

    def columns(o):
        return pl.ds(pl.multiple_of(o * depth, depth), depth)

    def grad_chunk(o):
        g = dot_nn(dlt, tok_ref[:, columns(o)])
        gbuf[o] = g[:cols] + g[cols:]

    turn = [pick(z, v) for v in ([3, 3, 0, 0], [2, 0, 3, 1], [1, 2, 1, 2], [0, 1, 2, 3])]
    origin = [pick(z, v) for v in ([1, 0, 3, 2], [2, 2, 1, 1], [3, 3, 0, 0])]

    for t in turn:
        grad_chunk(at(t, 1 - c))
        send(None, rc(gbuf.at[at(t, 1 - c)], pbuf.at[t], pr_s.at[t], pr_r.at[t], SIB))
    chain_d(z, upper, lower)
    for t in turn:
        grad_chunk(at(t))

    def pair_g(t):
        landed(pbuf.at[t], pr_r.at[t])
        gbuf[at(t)] += pbuf[t]

    def gather_g(t):
        @pl.when((t > z) & lower)
        def _():
            landed(rup.at[t], up_r.at[t])
            gbuf[at(t)] += rup[t]

        @pl.when((t < z) & upper)
        def _():
            landed(rdn.at[t], dn_r.at[t])
            gbuf[at(t)] += rdn[t]

    def send_g(t, cond):
        src = gbuf.at[at(t)]
        above, below = (t > z, t < z) if cond is None else (cond & (t > z), cond & (t < z))
        send(above, rc(src, rup.at[t], ch_s.at[t], up_r.at[t], {"fsdp": at(z + 1)}))
        send(below, rc(src, rdn.at[t], ch_s.at[t], dn_r.at[t], {"fsdp": at(z - 1)}))

    def spread_w(o_z):
        ref = wbuf.at[at(o_z), quarter]
        send(None, rc(ref, ref, nb_s.at[0, o_z], nb_r.at[0, o_z], XN))
        send(None, rc(ref, ref, nb_s.at[1, o_z], nb_r.at[1, o_z], YN))
        send(None, rc(ref, ref, sb_s.at[0, o_z], sb_r.at[0, o_z], SIB))

    def swap_w(o_z):
        ref = wbuf.at[at(o_z), xq]
        landed(ref, nb_r.at[0, o_z])
        part = wbuf.at[at(o_z), xq, pl.ds(0, half)]
        send(None, rc(part, part, nb_s.at[2, o_z], nb_r.at[2, o_z], YN))
        send(None, rc(ref, ref, sb_s.at[1, o_z], sb_r.at[1, o_z], SIB))
        ref2 = wbuf.at[at(o_z), yq]
        landed(ref2, nb_r.at[1, o_z])
        part2 = wbuf.at[at(o_z), yq, pl.ds(half, half)]
        send(None, rc(part2, part2, nb_s.at[3, o_z], nb_r.at[3, o_z], XN))
        send(None, rc(ref2, ref2, sb_s.at[2, o_z], sb_r.at[2, o_z], SIB))

    def last_w(o_z):
        landed(wbuf.at[at(o_z), dq, pl.ds(0, half)], nb_r.at[2, o_z])
        landed(wbuf.at[at(o_z), dq, pl.ds(half, half)], nb_r.at[3, o_z])
        ref = wbuf.at[at(o_z), dq]
        send(None, rc(ref, ref, sb_s.at[3, o_z], sb_r.at[3, o_z], SIB))

    def take_w(j):
        o_z = origin[j]
        landed(wbuf.at[at(o_z), quarter], cw_r.at[o_z])
        chain_w(o_z, (o_z < z) & upper, (o_z > z) & lower)
        spread_w(o_z)

    def take_d(j):
        o_z = origin[j]
        landed(dbuf.at[at(o_z)], cd_r.at[o_z])
        chain_d(o_z, (o_z < z) & upper, (o_z > z) & lower)

    def base_w(o):
        w = wbuf[o].reshape(depth, wbuf.shape[3])
        acc[...] += dot_nn(tok_ref[:, columns(o)], w)
        tgf[:, columns(o)] = dot_nt(cot_ref[...], w)

    def low_d(o):
        lacc[...] += dot_nt(dbuf[o], tok_ref[:, columns(o)])

    def tg_copy(o):
        return pltpu.make_async_copy(tg_ref.at[:, columns(o)], tg_out.at[:, columns(o)], tg_s.at[o])

    def back_d(o):
        d2 = dbuf[o]
        back = tgf[:, columns(o)] + (dot_nn(dlc[0], d2) + dot_nn(dlc[1], d2))
        tg_ref[:, columns(o)] = back.astype(bf16)
        tg_copy(o).start()

    ends = (z == 0) | (z == chips - 1)
    inner = jnp.logical_not(ends)
    acc[...] = jnp.zeros_like(acc)
    lacc[...] = jnp.zeros_like(lacc)
    take_w(0)
    pair_g(turn[0])
    send_g(turn[0], ends)
    take_w(1)
    base_w(me)
    swap_w(origin[0])
    take_w(2)
    gather_g(turn[0])
    send_g(turn[0], inner)
    low_d(me)
    swap_w(origin[1])
    take_d(0)
    low_d(at(origin[0]))
    landed(wbuf.at[sib], so_r)
    base_w(sib)
    pair_g(turn[1])
    gather_g(turn[1])
    send_g(turn[1], None)
    swap_w(origin[2])
    take_d(1)
    low_d(at(origin[1]))
    pair_g(turn[2])
    send_g(turn[2], ends)
    last_w(origin[0])
    base_w(at(origin[0]))
    last_w(origin[1])
    take_d(2)
    gather_g(turn[2])
    send_g(turn[2], inner)
    base_w(at(origin[1]))
    low_d(at(origin[2]))
    for zz in [z] + origin:
        landed(dbuf.at[at(zz, 1 - c)], sd_r.at[zz])
        low_d(at(zz, 1 - c))

    low_hi, low_lo = halves((lacc[:cols] + lacc[cols:]) * select)
    lowc = jnp.concatenate([low_hi.astype(f32), low_lo.astype(f32)], axis=0).T.astype(bf16)
    cot_t = cot.astype(f32).T.astype(bf16)
    fold = ubuf.shape[1]
    share = 2 * fold
    for f in range(n):
        u = dot_nn(cot_t[f * share : (f + 1) * share], lowc)
        u = u[:, :cols] + u[:, cols:]
        ubuf[f] = jnp.concatenate([u[:fold], u[fold:]], axis=1)
    for i in range(1, n):
        f = lax.rem(me + i, n)
        send(None, rc(ubuf.at[f], urecv.at[i], ug_s.at[i], ug_r.at[i], {"fsdp": f}))
    last_w(origin[2])
    acc[...] += dot_nn(lowc, jnp.concatenate([up_hi, up_hi], axis=0)) + dot_nn(
        lowc, jnp.concatenate([up_lo, up_lo], axis=0)
    )
    for o in (me, sib, at(origin[0]), at(origin[1])):
        back_d(o)
    base_w(at(origin[2]))
    back_d(at(origin[2]))
    for o_z in origin:
        for k, q in enumerate((quarter, xq, yq, dq)):
            landed(wbuf.at[at(o_z, 1 - c), q], sb_r.at[k, o_z])
        base_w(at(o_z, 1 - c))
        back_d(at(o_z, 1 - c))

    landed(pbuf.at[z], pr_r.at[z])
    dg_ref[...] = gbuf[me] + pbuf[z]

    @pl.when(lower)
    def _():
        landed(rup.at[z], up_r.at[z])
        dg_ref[...] += rup[z]

    @pl.when(upper)
    def _():
        landed(rdn.at[z], dn_r.at[z])
        dg_ref[...] += rdn[z]

    total = ubuf[me]
    for i in range(1, n):
        landed(urecv.at[i], ug_r.at[i])
        total = total + urecv[i]
    total = jnp.concatenate([total[:, :cols], total[:, cols:]], axis=0)
    ug_ref[...] = total.T
    proj_ref[...] = acc[...].astype(bf16)

    for o in range(n):
        tg_copy(o).wait()
    for cond, copy in sends:
        if cond is None:
            copy.wait_send()
        else:
            pl.when(cond)(copy.wait_send)


PIECES = 8


def write_kernel(*refs):
    ins, outs, held, sems = refs[:4], refs[4:8], refs[8:12], refs[12]
    ways = []
    for i in range(4):
        rows = ins[i].shape[0]
        pieces = PIECES if i == 1 else 1
        size = rows // pieces
        for p in range(pieces):
            part = pl.ds(p * size, size)
            k = len(ways)
            ways.append(
                (
                    pltpu.make_async_copy(ins[i].at[part], held[i].at[part], sems.at[0, k]),
                    pltpu.make_async_copy(held[i].at[part], outs[i].at[part], sems.at[1, k]),
                )
            )
    for way in ways:
        way[0].start()
    for way in ways:
        way[0].wait()
        way[1].start()
    for way in ways:
        way[1].wait()


def fused_step(chips, tokens, weight, downs, ups, tenants, slots, cotangent):
    rows, width = tokens.shape[1:]
    depth, out_width = weight.shape
    slot_count, rank = downs.shape[1], downs.shape[3]
    cols = slot_count * rank
    n = chips * CORES
    quarters = 4
    share = out_width // n
    down_t = jnp.transpose(downs[0], (0, 2, 1)).reshape(cols, depth)
    dma = pltpu.SemaphoreType.DMA
    vmem = pl.BlockSpec(memory_space=pltpu.VMEM)
    hbm = pl.BlockSpec(memory_space=pltpu.HBM)
    proj, tg, dg, ug = pl.pallas_call(
        functools.partial(step_kernel, chips, quarters, rank),
        out_shape=(
            jax.ShapeDtypeStruct((rows, out_width), bf16),
            jax.ShapeDtypeStruct((rows, width), bf16),
            jax.ShapeDtypeStruct((cols, depth), f32),
            jax.ShapeDtypeStruct((cols, share), f32),
        ),
        in_specs=[hbm] * 7,
        out_specs=(vmem, hbm, vmem, vmem),
        scratch_shapes=[
            pltpu.VMEM((n, quarters, depth // quarters, out_width), bf16),
            pltpu.VMEM((n, 2 * cols, depth), bf16),
            pltpu.VMEM((n, cols, depth), f32),
            pltpu.VMEM((chips, cols, depth), f32),
            pltpu.VMEM((chips, cols, depth), f32),
            pltpu.VMEM((chips, cols, depth), f32),
            pltpu.VMEM((n, share // 2, 2 * cols), f32),
            pltpu.VMEM((n, share // 2, 2 * cols), f32),
            pltpu.VMEM((2, rows, 2 * cols), bf16),
            pltpu.VMEM((rows, out_width), f32),
            pltpu.VMEM((2 * cols, rows), f32),
            dma((2, chips)),
            dma((chips,)),
            dma((2, chips)),
            dma((chips,)),
            dma((chips,)),
            dma((chips,)),
            dma((4, chips)),
            dma((4, chips)),
            dma((4, chips)),
            dma((4, chips)),
            dma,
            dma,
            dma((chips,)),
            dma((chips,)),
            dma((chips,)),
            dma((chips,)),
            dma((chips,)),
            dma((n,)),
            dma((n,)),
            dma((7,)),
            pltpu.VMEM((rows, width), bf16),
            pltpu.VMEM((cols, depth), f32),
            pltpu.VMEM((cols, out_width), f32),
            pltpu.SMEM(tenants.shape, jnp.int32),
            pltpu.SMEM(slots.shape, jnp.int32),
            pltpu.VMEM((rows, out_width), bf16),
            pltpu.VMEM((rows, width), f32),
            pltpu.VMEM((rows, width), bf16),
            dma((n,)),
        ],
        compiler_params=pltpu.CompilerParams(
            collective_id=0, has_side_effects=True, vmem_limit_bytes=63 * 1024 * 1024
        ),
        cost_estimate=pl.CostEstimate(
            flops=5 * rows * width * out_width, bytes_accessed=8 * 1024 * 1024, transcendentals=0
        ),
    )(
        tokens[0],
        weight.reshape(quarters, depth // quarters, out_width),
        down_t,
        ups[0].reshape(cols, out_width),
        tenants,
        slots,
        cotangent[0],
    )
    proj, tg, dg, ug = pl.pallas_call(
        write_kernel,
        out_shape=tuple(jax.ShapeDtypeStruct(x.shape, x.dtype) for x in (proj, tg, dg, ug)),
        in_specs=[pl.BlockSpec(memory_space=pl.ANY)] * 4,
        out_specs=(hbm,) * 4,
        scratch_shapes=[pltpu.VMEM(x.shape, x.dtype) for x in (proj, tg, dg, ug)]
        + [dma((2, PIECES + 3))],
        compiler_params=pltpu.CompilerParams(vmem_limit_bytes=63 * 1024 * 1024),
        cost_estimate=pl.CostEstimate(flops=0, bytes_accessed=4 * rows * width, transcendentals=0),
    )(proj, tg, dg, ug)
    down_gradient = jnp.transpose(dg.reshape(slot_count, rank, depth), (0, 2, 1))[None]
    up_gradient = jnp.transpose(ug.reshape(slot_count, rank, share), (0, 2, 1))[None]
    return proj[None], tg[None], down_gradient, up_gradient


def solution(mesh):
    sizes = (mesh.shape["rep"], mesh.shape["fsdp"], mesh.shape["adapt"], mesh.shape["sub"])
    body = functools.partial(fused_step, sizes[1] // CORES) if sizes == (2, 8, 2, 1) else per_device
    in_specs = (
        P("adapt", ("rep", "fsdp", "sub"), None),
        P("fsdp", None),
        P("adapt", "rep", "fsdp", None),
        P("adapt", "rep", None, None),
        P("adapt", ("rep", "fsdp", "sub")),
        P("adapt", "rep"),
        P("adapt", ("rep", "fsdp", "sub"), None),
    )
    out_specs = (
        P("adapt", ("rep", "fsdp", "sub"), None),
        P("adapt", ("rep", "fsdp", "sub"), None),
        P("adapt", "rep", ("fsdp", "sub"), None),
        P("adapt", "rep", ("fsdp", "sub"), None),
    )
    return jax.shard_map(
        body, mesh=mesh, in_specs=in_specs, out_specs=out_specs, check_vma=False
    )
```
